32 devices in a mesh: node: 8 (over z, x), sector: 4 (over y, core).
Axes of the slice: x: 2, y: 2, z: 4, core: 2. Of those that a mesh axis runs over, the one named last changes fastest.
Arguments:
- returns: bfloat16 [1024, 12, 2048], P('node'), may hold values from -0.29882812 to 0.29882812
- barrier_scale: float32 [1024, 12], P('node'), may hold values from 0.25 to 4
- parent_ids: int32 [1024, 1], P('node'), may hold values from 0 to 7; in each aligned block of 128 rows (0 to 127, 128 to 255, ...) at most 32 rows name the same one
- loadings: float32 [8, 2048], P('node'), may hold values from -3 to 3
- own_variance: float32 [8, 2048], P('node'), may hold values from 0.5 to 4
- sector_sizes: int32 [64], replicated, may hold values from 1 to 64, 2048 in all
Outputs:
- cholesky_rows: float32 [8, 2048, 2048], P('node', 'sector')
The draws below stay inside these ranges and needn't reach their ends.
Inputs may be any that keep to these rules, and one draw needn't show every extreme that they name: `parent_ids`: of the 128 children held by one index of node (aligned blocks of rows), at most 32 share a parent; in every draw some block has exactly 32 children of one parent. `sector_sizes`: the sizes sum to 2048, and the largest is 64.
All inputs are finite; a program needn't handle non-finite values.
Results may differ from the reference program's by a relative error of at most 0.00045.
Values may be sent and summed in bfloat16 or wider, within the bound.
No kernel may reach another device: no remote copies, remote signals or barrier semaphores. Data moves between devices by JAX's collectives and lax.ppermute only.
A program may use at most 192 MiB of HBM per device.

```python
import math
import jax
import jax.numpy as jnp
import numpy as np
from jax import lax

N = 2048
SECT = 64
SECMAX = 64
K = 12
CHILD_DEV = 128
CAP = 32
PARENTS = 8
CHILDREN = 1024
N_NODE = 8


def level_of(key, dims, shards, low, high):
    def one(axis_at, parts):
        draws = jax.random.uniform(jax.random.fold_in(jax.random.fold_in(key, 6), axis_at), (parts,), jnp.float32, low / len(shards), high / len(shards))
        return jnp.repeat(jnp.exp(draws), dims[axis_at] // parts).reshape((-1,) + (1,) * (len(dims) - axis_at - 1))

    factor_of = one(*shards[0])
    for cut in shards[1:]:
        factor_of = factor_of * one(*cut)
    return factor_of


def profile(count, total, bound, skew):
    weights = [(1 << 20) // math.isqrt(grade ** skew) + 1 for grade in range(2, count + 1)]
    rest, holding = total - bound - (count - 1), [1] * (count - 1)
    while rest > 0:
        candidates = [i for i in range(count - 1) if holding[i] < bound]
        pool, remaining = sum([weights[i] for i in candidates]), rest
        for i in candidates:
            more = min(bound - holding[i], max(1, remaining * weights[i] // pool), rest)
            holding[i] = holding[i] + more
            rest = rest - more
    return np.array([bound] + holding)


def uneven(own_key, count, total, bound, lean):
    if count == 2:
        one = jax.random.randint(own_key, (), max(1, total - bound), min(bound, total - 1) + 1)
        return jnp.stack([one, total - one])
    tallies = jnp.asarray(profile(count, total, bound, lean), jnp.int32)
    pairs = (count - 1) // 2
    donor, taker = tallies[1:1 + 2 * pairs:2], tallies[2:2 + 2 * pairs:2]
    slack = jnp.minimum(donor - 1, bound - taker)
    moved = jax.random.randint(jax.random.fold_in(own_key, 1), (pairs,), 0, 1 << 20) % (slack + 1)
    tallies = tallies.at[1:1 + 2 * pairs:2].set(donor - moved).at[2:2 + 2 * pairs:2].set(taker + moved)
    return tallies[jax.random.permutation(jax.random.fold_in(own_key, 2), count)]


def routed_block(own_key, own, number, rows, amount, top, bound, slope):
    ranking = jax.random.permutation(own_key, amount)
    crowded, usual = portions_of(amount, rows * top, bound, slope, True), portions_of(amount, rows * top, bound, slope, False)
    places = jnp.arange(amount)

    def named(tallies, offset_by):
        used = int((tallies > 0).sum())
        fixed = max(1, used // 4)
        passed = fixed + (places - fixed + offset_by * (used - fixed)) % max(1, amount - fixed)
        return jnp.zeros((amount,), jnp.int32).at[ranking[jnp.where(places < fixed, places, passed)]].set(jnp.asarray(tallies, jnp.int32))

    tallies = jnp.where(number % 4 == 0, named(crowded, number // 4), named(usual, number - number // 4 - 1))
    mixed = jax.random.permutation(jax.random.fold_in(own, 3), amount)
    source_of, sink = mixed[0:amount // 2 * 2:2], mixed[1:amount // 2 * 2:2]
    slack = jnp.minimum(tallies[source_of] - 1, bound - tallies[sink]) // 2
    slack = jnp.where((source_of == ranking[0]) | (sink == ranking[0]) | (tallies[sink] == 0), 0, jnp.maximum(slack, 0))
    passed = jax.random.randint(jax.random.fold_in(own, 4), (amount // 2,), 0, 1 << 20) % (slack + 1)
    tallies = tallies.at[source_of].add(-passed).at[sink].add(passed)
    members = jnp.searchsorted(jnp.cumsum(tallies), jnp.arange(rows * top), side="right").astype(jnp.int32)
    listing = members.reshape(top, rows).T
    listing = listing[jax.random.permutation(jax.random.fold_in(own, 1), rows)]
    offset_by = jax.random.randint(jax.random.fold_in(own, 2), (rows, 1), 0, top)
    return jnp.take_along_axis(listing, (jnp.arange(top)[None, :] + offset_by) % top, axis=1)


def portions_of(count, total, reach, lean, full):
    portions = [(1 << 20) // math.isqrt(standing ** lean) + 1 for standing in range(1, count + 1)]
    largest = reach if full else min(reach, max(-(-total // count), total * portions[0] // sum(portions)))
    least = 1 if total - largest >= count - 1 else 0
    given, rest = [largest] + [least] * (count - 1), total - largest - least * (count - 1)
    while rest > 0:
        movable = [i for i in range(1, count) if given[i] < largest] or [i for i in range(1, count) if given[i] < reach]
        whole, left = sum([portions[i] for i in movable]), rest
        for i in movable:
            more = min(reach - given[i], max(1, left * portions[i] // whole), rest)
            given[i] = given[i] + more
            rest = rest - more
    return np.array(given)


def scatter_about(stream_key, dims, scale, limit, pieces=(), kind=jnp.bfloat16):
    drawn = scale * jax.random.normal(stream_key, dims, jnp.float32)
    if pieces:
        drawn = drawn * level_of(stream_key, dims, pieces, -0.22, 0.18)
    return jnp.clip(drawn, -limit, limit).astype(kind)


def setup_inputs(seed: int = 0) -> dict:
    streams_of = jax.random.split(jax.random.key(seed), 7)
    returns = scatter_about(streams_of[0], (CHILDREN, K, N), 0.05, 0.29882812, ((0, 8),))
    barrier_scale = jnp.clip(jnp.exp(math.log(4.0) - 2.7725887 * jax.random.uniform(streams_of[1], (CHILDREN, K), jnp.float32) ** level_of(streams_of[1], (CHILDREN, K), ((0, 8),), -0.2, 0.2)), 0.25, 4.0)
    parent_ids_keys = jax.random.split(jax.random.fold_in(streams_of[2], 1), CHILDREN // CHILD_DEV)
    parent_ids_turns = jax.random.permutation(jax.random.fold_in(streams_of[2], 3), CHILDREN // CHILD_DEV)
    parent_ids = jax.vmap(lambda own, number: routed_block(jax.random.fold_in(streams_of[2], 2), own, number, CHILD_DEV, PARENTS, 1, CAP, 2))(parent_ids_keys, parent_ids_turns).reshape((CHILDREN, 1))
    loadings = scatter_about(streams_of[3], (PARENTS, N), 0.5, 3.0, ((0, 8),), jnp.float32)
    own_variance = jnp.clip(jnp.exp(math.log(4.0) - 2.0794415 * jax.random.uniform(streams_of[4], (PARENTS, N), jnp.float32) ** level_of(streams_of[4], (PARENTS, N), ((0, 8),), -0.2, 0.2)), 0.5, 4.0)
    sector_sizes = uneven(streams_of[5], SECT, N, SECMAX, 1).astype(jnp.int32)
    return dict(returns=returns, barrier_scale=barrier_scale, parent_ids=parent_ids, loadings=loadings, own_variance=own_variance, sector_sizes=sector_sizes)


def sector_labels(sector_sizes, count):
    sector_ends = jnp.cumsum(sector_sizes).astype(jnp.int32)
    asset_index = jnp.arange(count, dtype=jnp.int32)
    return lax.optimization_barrier(jnp.sum((asset_index[:, None] >= sector_ends[None, :]).astype(jnp.int32), axis=1))

def reference(returns, barrier_scale, parent_ids, loadings, own_variance, sector_sizes):
    scaled = (jnp.sqrt(barrier_scale)[:, :, None] * returns.astype(jnp.float32)).astype(jnp.bfloat16)
    targets = parent_ids[:, 0].astype(jnp.int32)
    by_parent = jnp.argsort(targets, stable=True).astype(jnp.int32)
    parent_index = jnp.arange(PARENTS, dtype=jnp.int32)
    counts = lax.optimization_barrier(jnp.sum((targets[None, :] == parent_index[:, None]).astype(jnp.int32), axis=1))
    starts = (jnp.cumsum(counts) - counts).astype(jnp.int32)
    sector_of = sector_labels(sector_sizes, N)
    same_sector = sector_of[:, None] == sector_of[None, :]
    slot_count = N_NODE * CAP

    def factor_parent(parent):
        slots = jnp.arange(slot_count, dtype=jnp.int32)
        chosen = jnp.clip(starts[parent] + slots, 0, CHILDREN - 1).astype(jnp.int32)
        filled = slots < counts[parent]
        picked = scaled[by_parent[chosen]].astype(jnp.float32)
        picked = jnp.where(filled[:, None, None], picked, jnp.zeros((), jnp.float32))
        gathered_rows = picked.reshape(slot_count * K, N)
        schur = jnp.dot(gathered_rows.T.astype(jnp.float32), gathered_rows.astype(jnp.float32), precision=lax.Precision.HIGHEST, preferred_element_type=jnp.float32)
        loading = loadings[parent]
        covariance = jnp.where(same_sector, loading[:, None] * loading[None, :], jnp.zeros((), jnp.float32))
        normal_matrix = schur + covariance + jnp.diag(own_variance[parent])
        return jnp.linalg.cholesky(normal_matrix)
    return lax.map(factor_parent, parent_index)
```

```python
import functools
import jax
import jax.numpy as jnp
from jax import lax
from jax.experimental import pallas as pl
from jax.experimental.pallas import tpu as pltpu
from jax.sharding import PartitionSpec as P

F32 = jnp.float32
BF16 = jnp.bfloat16
LANES = 128
BLOCK = 128
HALF = 64
VMEM_LIMIT = 56 * 2**20


def split(x):
    high = x.astype(BF16)
    return high, (x - high.astype(F32)).astype(BF16)


def dot3(a, b, dims):
    one = lambda x, y: lax.dot_general(x, y, (dims, ((), ())), preferred_element_type=F32)
    (ah, al), (bh, bl) = a, b
    return one(ah, bh) + (one(ah, bl) + one(al, bh))


NT = ((1,), (1,))
TN = ((0,), (0,))
NN = ((1,), (0,))


def sweep_rows(rows_in, first, comb, rout):
    n = rows_in[0].shape[1]
    lane = lax.broadcasted_iota(jnp.int32, (8, n), 1)
    sub = lax.broadcasted_iota(jnp.int32, (8, n), 0)
    rows = list(rows_in)
    of_row = lambda v, i: jnp.broadcast_to(v[i : i + 1, :], (8, n))
    of_lane = lambda v, j: jnp.take_along_axis(v, jnp.full((8, n), j, jnp.int32), axis=1)
    for g in range(len(rows)):
        o = first + 8 * g
        cur = rows[g]
        cols = [of_lane(cur, o + j) for j in range(8)]
        in_group = (lane >= o) & (lane < o + 8)
        raw = cur
        aug = jnp.where(in_group, jnp.where(lane == o + sub, 1.0, 0.0), cur)
        w_rows = r_rows = None
        for x in range(0, 8, 2):
            y = x + 1
            a, b, c = of_row(cols[x], x), of_row(cols[y], x), of_row(cols[y], y)
            inv_det = pltpu.reciprocal(a * c - b * b, approx=True)
            cx = jnp.where(sub == x, -1.0, jnp.where(sub == y, 0.0, cols[x]))
            cy = jnp.where(sub == y, -1.0, jnp.where(sub == x, 0.0, cols[y]))
            mx, my = inv_det * (c * cx - b * cy), inv_det * (a * cy - b * cx)
            pair = (sub == x) | (sub == y)
            for l in range(y + 1, 8):
                cols[l] = jnp.where(pair, 0.0, cols[l]) - (
                    mx * of_row(cols[l], x) + my * of_row(cols[l], y)
                )
            ra = lax.rsqrt(a)
            bra = b * ra
            rc = lax.rsqrt(c - bra * bra)
            scale = jnp.where(sub == x, ra, rc)
            back = jnp.where(sub == x, 0.0, bra) * ra
            ax, ay, rx, ry = of_row(aug, x), of_row(aug, y), of_row(raw, x), of_row(raw, y)
            wn = (aug - back * ax) * scale
            rn = (raw - back * rx) * scale
            w_rows = wn if w_rows is None else jnp.where(sub >= x, wn, w_rows)
            r_rows = rn if r_rows is None else jnp.where(sub >= x, rn, r_rows)
            aug = jnp.where(pair, 0.0, aug) - (mx * ax + my * ay)
            raw = raw - (mx * rx + my * ry)
        comb[o : o + 8, :] = w_rows
        rout[o : o + 8, :] = jnp.where(lane >= o, r_rows, 0.0)
        solved = [of_row(aug, j) for j in range(8)]
        for h in range(g + 1, len(rows)):
            acc = [None, None]
            for j in range(8):
                t = of_lane(rows[h], o + j) * solved[j]
                acc[j % 2] = t if acc[j % 2] is None else acc[j % 2] + t
            rows[h] = jnp.where(in_group, 0.0, rows[h]) - (acc[0] + acc[1])


def factor_block(rest, comb, rout):
    n = BLOCK
    sweep_rows([rest[8 * h : 8 * h + 8, :] for h in range(HALF // 8)], 0, comb, rout)
    row = lax.broadcasted_iota(jnp.int32, (HALF, n), 0)
    lane = lax.broadcasted_iota(jnp.int32, (HALF, n), 1)
    top = jnp.where((lane < HALF) & (lane > row), 0.0, comb[0:HALF, :])
    low = jnp.where(lane < HALF, 0.0, rest[HALF:n, :])
    th, tl = split(top)
    low = low - dot3((th[:, HALF:], tl[:, HALF:]), (th, tl), TN)
    sweep_rows([low[8 * h : 8 * h + 8, :] for h in range(HALF // 8)], HALF, comb, rout)
    row = lax.broadcasted_iota(jnp.int32, (n, n), 0)
    lane = lax.broadcasted_iota(jnp.int32, (n, n), 1)
    return jnp.where(lane <= row, comb[...], 0.0)


def band_kernel(off, width, prior, *refs):
    count = len(prior)
    it = iter(refs)
    take = lambda k: [next(it) for _ in range(k)]
    (label_row, load_row, label_col, load_col, var_col) = take(5)
    x_hbm = take(count + 1)
    lh_hbm, ll_hbm = take(max(count - 1, 0)), take(max(count - 1, 0))
    ih_hbm, il_hbm = take(count), take(count)
    lfull, lh_out, ll_out, ih_out, il_out = take(5)
    x_mine, x_other, lh, ll, ih, il, mat, ph, pl_, diag, comb, rout, sems = take(13)

    def copy(src, dst, k):
        return pltpu.make_async_copy(src, dst, sems.at[k])

    mine = copy(x_hbm[count], x_mine, 0)
    mine.start()
    others = [copy(x_hbm[j], x_other.at[j], 1 + j) for j in range(count)]
    for c in others:
        c.start()
    later = []
    for j in range(count):
        o, w = prior[j]
        if j > 0:
            later.append(copy(lh_hbm[j - 1], lh.at[pl.ds(o, w), pl.ds(0, o)], 1 + count + 4 * j))
            later.append(copy(ll_hbm[j - 1], ll.at[pl.ds(o, w), pl.ds(0, o)], 2 + count + 4 * j))
        later.append(copy(ih_hbm[j], ih.at[j], 3 + count + 4 * j))
        later.append(copy(il_hbm[j], il.at[j], 4 + count + 4 * j))
    for c in later:
        c.start()
    mine.wait()

    def normal_part(x, o, w):
        gram = lax.dot_general(x_mine[...], x, (NT, ((), ())), preferred_element_type=F32)
        same = label_col[...] == label_row[:, o : o + w]
        return gram + jnp.where(same, load_col[...] * load_row[:, o : o + w], 0.0)

    for j in range(count):
        o, w = prior[j]
        others[j].wait()
        mat[:, o : o + w] = normal_part(x_other[j], o, w)
    on_diag = lax.broadcasted_iota(jnp.int32, (width, width), 0) == lax.broadcasted_iota(
        jnp.int32, (width, width), 1
    )
    diag[...] = normal_part(x_mine[...], off, width) + jnp.where(on_diag, var_col[...], 0.0)
    for c in later:
        c.wait()
    for j in range(count):
        o, w = prior[j]
        acc = mat[:, o : o + w]
        if j > 0:
            acc = acc - dot3(
                (ph[:, :o], pl_[:, :o]), (lh[o : o + w, :o], ll[o : o + w, :o]), NT
            )
        part = dot3(split(acc), (ih[j], il[j]), NT)
        lfull[:, o : o + w] = part
        ph[:, o : o + w], pl_[:, o : o + w] = split(part)
    if count:
        lh_out[...] = ph[...]
        ll_out[...] = pl_[...]
        diag[...] = diag[...] - dot3((ph[...], pl_[...]), (ph[...], pl_[...]), NT)
    lfull[:, off : off + width] = jnp.zeros((width, width), F32)
    rest = lfull.shape[1] - off - width
    if rest:
        lfull[:, off + width :] = jnp.zeros((width, rest), F32)
    ih_out[...] = jnp.zeros((width, width), BF16)
    il_out[...] = jnp.zeros((width, width), BF16)

    row = lax.broadcasted_iota(jnp.int32, (width, BLOCK), 0)

    def step(k, carry):
        at = pl.multiple_of(k * BLOCK, BLOCK)
        here = pl.ds(at, BLOCK)
        w = factor_block(diag[here, here], comb, rout)
        wh, wl = split(w)
        column = dot3(split(diag[:, here]), (wh, wl), NT)
        column = jnp.where(row >= at + BLOCK, column, 0.0)
        ch, cl = split(column)
        diag[...] = diag[...] - dot3((ch, cl), (ch, cl), NT)
        out_at = pl.ds(pl.multiple_of(off + at, BLOCK), BLOCK)
        lfull[:, out_at] = column
        lfull[here, out_at] = jnp.transpose(rout[...])
        lh_k, ll_k = split(lfull[here, off : off + width])
        cols = lax.broadcasted_iota(jnp.int32, (BLOCK, width), 1)
        lh_k = jnp.where(cols < at, lh_k, jnp.zeros_like(lh_k))
        ll_k = jnp.where(cols < at, ll_k, jnp.zeros_like(ll_k))
        below = -dot3((lh_k, ll_k), (ih_out[...], il_out[...]), NN)
        rows = dot3((wh, wl), split(below), NN)
        ih_out[here, :], il_out[here, :] = split(rows)
        ih_out[here, here], il_out[here, here] = wh, wl
        return carry

    lax.fori_loop(0, width // BLOCK, step, 0)


def band(off, width, total, prior, vectors, xs, lhs, lls, ihs, ils):
    count = len(prior)
    depth = xs[0].shape[1]
    label_row, load_row, label_col, load_col, var_col = vectors
    any_spec = pl.BlockSpec(memory_space=pl.ANY)
    vm = pl.BlockSpec(memory_space=pltpu.VMEM)
    rows_of = lambda v: v[off : off + width]
    args = [label_row, load_row, rows_of(label_col), rows_of(load_col), rows_of(var_col)]
    in_specs = [vm] * 5
    big = list(xs) + list(lhs[1:]) + list(lls[1:]) + list(ihs) + list(ils)
    args += big
    in_specs += [any_spec] * len(big)
    left = max(off, BLOCK)
    slots = max(count, 1)
    widest = max([w for _, w in prior] + [BLOCK])
    return pl.pallas_call(
        functools.partial(band_kernel, off, width, prior),
        out_shape=[
            jax.ShapeDtypeStruct((width, total), F32),
            jax.ShapeDtypeStruct((width, left), BF16),
            jax.ShapeDtypeStruct((width, left), BF16),
            jax.ShapeDtypeStruct((width, width), BF16),
            jax.ShapeDtypeStruct((width, width), BF16),
        ],
        in_specs=in_specs,
        out_specs=[vm] * 5,
        scratch_shapes=[
            pltpu.VMEM((width, depth), BF16),
            pltpu.VMEM((slots, widest, depth), BF16),
            pltpu.VMEM((left, left), BF16),
            pltpu.VMEM((left, left), BF16),
            pltpu.VMEM((slots, widest, widest), BF16),
            pltpu.VMEM((slots, widest, widest), BF16),
            pltpu.VMEM((width, left), F32),
            pltpu.VMEM((width, left), BF16),
            pltpu.VMEM((width, left), BF16),
            pltpu.VMEM((width, width), F32),
            pltpu.VMEM((BLOCK, BLOCK), F32),
            pltpu.VMEM((BLOCK, BLOCK), F32),
            pltpu.SemaphoreType.DMA((8 + 5 * slots,)),
        ],
        compiler_params=pltpu.CompilerParams(vmem_limit_bytes=VMEM_LIMIT),
        name="band_%d" % off,
    )(*args)


def gather_kernel(rows_per, capacity, info, slots, returns, scale, out, stage):
    dests = out.shape[0]

    def one(d, carry):
        for s in range(capacity):
            child = slots[d * capacity + s]
            keep = jnp.where(child >= 0, 1.0, 0.0).astype(F32)
            at = jnp.maximum(child, 0)
            value = returns[at].astype(F32) * (scale[at] * keep)
            stage[s * rows_per : (s + 1) * rows_per, :] = value
        out[d] = jnp.transpose(stage[...]).astype(BF16)
        return carry

    lax.fori_loop(0, dests, one, 0)


def gather(returns, scale, slots, column_block, dests, capacity):
    children, rows_per, _ = returns.shape
    depth = capacity * rows_per
    grid_spec = pltpu.PrefetchScalarGridSpec(
        num_scalar_prefetch=2,
        grid=(1,),
        in_specs=[
            pl.BlockSpec((children, rows_per, LANES), lambda i, info, slots: (0, 0, info[0])),
            pl.BlockSpec((children, rows_per, LANES), lambda i, info, slots: (0, 0, 0)),
        ],
        out_specs=pl.BlockSpec((dests, LANES, depth), lambda i, info, slots: (0, 0, 0)),
        scratch_shapes=[pltpu.VMEM((depth, LANES), F32)],
    )
    return pl.pallas_call(
        functools.partial(gather_kernel, rows_per, capacity),
        out_shape=jax.ShapeDtypeStruct((dests, LANES, depth), BF16),
        grid_spec=grid_spec,
        compiler_params=pltpu.CompilerParams(vmem_limit_bytes=VMEM_LIMIT),
        name="gather",
    )(column_block, slots, returns, scale)


def on_device(returns, barrier_scale, parent_ids, loadings, own_variance, sector_sizes):
    node_count = lax.axis_size("node")
    sector_count = lax.axis_size("sector")
    my_index = lax.axis_index("sector")
    child_count, row_count, asset_count = returns.shape
    capacity = max(2, 2 * child_count // node_count)
    band_rows = asset_count // sector_count
    targets = parent_ids[:, 0]
    child_index = jnp.arange(child_count, dtype=jnp.int32)
    earlier = (targets[:, None] == targets[None, :]) & (child_index[None, :] < child_index[:, None])
    position = jnp.sum(earlier.astype(jnp.int32), axis=1)
    slot_of = targets * capacity + position
    slot_index = jnp.arange(node_count * capacity, dtype=jnp.int32)
    slots = jnp.max(
        jnp.where(slot_of[None, :] == slot_index[:, None], child_index[None, :], -1), axis=1
    )
    scale = jnp.broadcast_to(jnp.sqrt(barrier_scale)[:, :, None], (child_count, row_count, LANES))

    sector_ends = jnp.cumsum(sector_sizes)
    asset_index = jnp.arange(asset_count, dtype=jnp.int32)
    labels = jnp.sum((asset_index[:, None] >= sector_ends[None, :]).astype(jnp.int32), axis=1)
    vectors = (
        labels[None, :],
        loadings,
        labels[:, None],
        loadings[0][:, None],
        own_variance[0][:, None],
    )

    width = sector_count * LANES
    prior, xs, lhs, lls, ihs, ils, bands = [], [], [], [], [], [], []
    for off in range(0, asset_count, width):
        block = (off // LANES + my_index)[None].astype(jnp.int32)
        outbox = gather(returns, scale, slots, block, node_count, capacity)
        arrived = lax.all_to_all(outbox, "node", split_axis=0, concat_axis=0, tiled=True)
        inbox = lax.all_gather(arrived, "sector", axis=0)
        x = inbox.transpose(0, 2, 1, 3).reshape(width, -1)
        xs.append(x)
        full, lh, ll, ih, il = band(
            off, width, asset_count, tuple(prior), vectors, xs, lhs, lls, ihs, ils
        )
        prior.append((off, width))
        bands.append(full)
        lhs.append(lh)
        lls.append(ll)
        ihs.append(ih)
        ils.append(il)
    rows = jnp.concatenate(bands, axis=0)
    return lax.dynamic_slice_in_dim(rows, my_index * band_rows, band_rows, 0)[None]


def solution(mesh):
    in_specs = (
        P("node", None, None),
        P("node", None),
        P("node", None),
        P("node", None),
        P("node", None),
        P(),
    )
    out_specs = P("node", "sector", None)
    return jax.shard_map(
        on_device, mesh=mesh, in_specs=in_specs, out_specs=out_specs, check_vma=False
    )
```

```python
import functools
import jax
import jax.numpy as jnp
from jax import lax
from jax.experimental import pallas as pl
from jax.experimental.pallas import tpu as pltpu
from jax.sharding import PartitionSpec as P

F32 = jnp.float32
BF16 = jnp.bfloat16
LANES = 128
BLOCK = 128
HALF = 64
VMEM_LIMIT = 28 * 2**20
GROUPS = 2
LEAD = 9
GATHER_LIMIT = 62 * 2**20


def split(x):
    high = x.astype(BF16)
    return high, (x - high.astype(F32)).astype(BF16)


def dot3(a, b, dims):
    one = lambda x, y: lax.dot_general(x, y, (dims, ((), ())), preferred_element_type=F32)
    (ah, al), (bh, bl) = a, b
    return one(ah, bh) + (one(ah, bl) + one(al, bh))


NT = ((1,), (1,))
TN = ((0,), (0,))
NN = ((1,), (0,))


def sweep_rows(rows_in, first, comb, rout):
    n = rows_in[0].shape[1]
    lane = lax.broadcasted_iota(jnp.int32, (8, n), 1)
    sub = lax.broadcasted_iota(jnp.int32, (8, n), 0)
    rows = list(rows_in)
    of_row = lambda v, i: jnp.broadcast_to(v[i : i + 1, :], (8, n))
    of_lane = lambda v, j: jnp.take_along_axis(v, jnp.full((8, n), j, jnp.int32), axis=1)
    for g in range(len(rows)):
        o = first + 8 * g
        cur = rows[g]
        cols = [of_lane(cur, o + j) for j in range(8)]
        in_group = (lane >= o) & (lane < o + 8)
        raw = cur
        aug = jnp.where(in_group, jnp.where(lane == o + sub, 1.0, 0.0), cur)
        w_rows = r_rows = None
        for x in range(0, 8, 2):
            y = x + 1
            a, b, c = of_row(cols[x], x), of_row(cols[y], x), of_row(cols[y], y)
            inv_det = pltpu.reciprocal(a * c - b * b, approx=True)
            cx = jnp.where(sub == x, -1.0, jnp.where(sub == y, 0.0, cols[x]))
            cy = jnp.where(sub == y, -1.0, jnp.where(sub == x, 0.0, cols[y]))
            mx, my = inv_det * (c * cx - b * cy), inv_det * (a * cy - b * cx)
            pair = (sub == x) | (sub == y)
            for l in range(y + 1, 8):
                cols[l] = jnp.where(pair, 0.0, cols[l]) - (
                    mx * of_row(cols[l], x) + my * of_row(cols[l], y)
                )
            ra = lax.rsqrt(a)
            bra = b * ra
            rc = lax.rsqrt(c - bra * bra)
            scale = jnp.where(sub == x, ra, rc)
            back = jnp.where(sub == x, 0.0, bra) * ra
            ax, ay, rx, ry = of_row(aug, x), of_row(aug, y), of_row(raw, x), of_row(raw, y)
            wn = (aug - back * ax) * scale
            rn = (raw - back * rx) * scale
            w_rows = wn if w_rows is None else jnp.where(sub >= x, wn, w_rows)
            r_rows = rn if r_rows is None else jnp.where(sub >= x, rn, r_rows)
            aug = jnp.where(pair, 0.0, aug) - (mx * ax + my * ay)
            raw = raw - (mx * rx + my * ry)
        comb[o : o + 8, :] = w_rows
        rout[o : o + 8, :] = jnp.where(lane >= o, r_rows, 0.0)
        solved = [of_row(aug, j) for j in range(8)]
        for h in range(g + 1, len(rows)):
            acc = [None, None]
            for j in range(8):
                t = of_lane(rows[h], o + j) * solved[j]
                acc[j % 2] = t if acc[j % 2] is None else acc[j % 2] + t
            rows[h] = jnp.where(in_group, 0.0, rows[h]) - (acc[0] + acc[1])


def factor_block(rest, comb, rout):
    n = BLOCK
    sweep_rows([rest[8 * h : 8 * h + 8, :] for h in range(HALF // 8)], 0, comb, rout)
    row = lax.broadcasted_iota(jnp.int32, (HALF, n), 0)
    lane = lax.broadcasted_iota(jnp.int32, (HALF, n), 1)
    top = jnp.where((lane < HALF) & (lane > row), 0.0, comb[0:HALF, :])
    low = jnp.where(lane < HALF, 0.0, rest[HALF:n, :])
    th, tl = split(top)
    low = low - dot3((th[:, HALF:], tl[:, HALF:]), (th, tl), TN)
    sweep_rows([low[8 * h : 8 * h + 8, :] for h in range(HALF // 8)], HALF, comb, rout)
    row = lax.broadcasted_iota(jnp.int32, (n, n), 0)
    lane = lax.broadcasted_iota(jnp.int32, (n, n), 1)
    return jnp.where(lane <= row, comb[...], 0.0)


def band_kernel(plan, at_band, at_share, masks, *refs):
    prior, (off, width) = plan[:at_band], plan[at_band]
    count, last = at_band, at_band + 1 == len(plan)
    it = iter(refs)
    take = lambda k: [next(it) for _ in range(k)]
    (vectors,) = take(1)
    out_in = take(1 if count else 0)
    xs = take(count)
    piece_hbm = take(len(masks))
    lhs, lls = [None] + take(max(count - 1, 0)), [None] + take(max(count - 1, 0))
    ihs, ils = take(count), take(count)
    (out,) = take(1)
    x_mine, ph, pl_, ih_out, il_out = take(5)
    mat, diag, cur, wh, wl, comb, rout, rprev, full, sems = take(10)
    me = lax.axis_index("sector")
    used = [0]

    def copy(src, dst):
        c = pltpu.make_async_copy(src, dst, sems.at[used[0]])
        used[0] += 1
        return c

    mine = []
    for ref, mask in zip(piece_hbm, masks):
        if mask is None:
            mine.append(copy(ref, x_mine))
        else:
            parts, part_depth = ref.shape[0], ref.shape[2]
            rows = width // lax.axis_size("sector")
            to = pl.ds(pl.multiple_of((me ^ mask) * rows, rows), rows)
            for d in range(parts):
                src = ref.at[d, pl.ds(at_share, rows)]
                mine.append(copy(src, x_mine.at[to, pl.ds(d * part_depth, part_depth)]))
    for c in mine:
        c.start()
    for c in mine:
        c.wait()

    turned = jnp.concatenate(
        [jnp.transpose(vectors[:, o : o + BLOCK]) for o in range(off, off + width, BLOCK)]
    )
    label_col, load_col, var_col = turned[:, 0:1], turned[:, 1:2], turned[:, 2:3]

    def normal_part(x, o, w):
        gram = lax.dot_general(x_mine[...], x, (NT, ((), ())), preferred_element_type=F32)
        same = label_col == vectors[0:1, o : o + w]
        return gram + jnp.where(same, load_col * vectors[1:2, o : o + w], 0.0)

    on_diag = lax.broadcasted_iota(jnp.int32, (width, width), 0) == lax.broadcasted_iota(
        jnp.int32, (width, width), 1
    )
    diag[...] = normal_part(x_mine[...], off, width) + jnp.where(on_diag, var_col, 0.0)
    for j in range(count):
        o, w = prior[j]
        mat[:, o : o + w] = normal_part(xs[j][...], o, w)
    for j in range(count):
        o, w = prior[j]
        acc = mat[:, o : o + w]
        if j > 0:
            acc = acc - dot3((ph[:, :o], pl_[:, :o]), (lhs[j][...], lls[j][...]), NT)
        part = dot3(split(acc), (ihs[j][...], ils[j][...]), NT)
        full[:, o : o + w] = part
        ph[:, o : o + w], pl_[:, o : o + w] = split(part)
    if count:
        diag[...] = diag[...] - dot3((ph[...], pl_[...]), (ph[...], pl_[...]), NT)

    total, band_rows = full.shape[1], out.shape[0]
    results = []
    for r in range(off // band_rows, (off + width - 1) // band_rows + 1):
        low, high = max(off, r * band_rows), min(off + width, (r + 1) * band_rows)
        src, dst = pl.ds(low - off, high - low), pl.ds(low - r * band_rows, high - low)
        part = lambda o, w: copy(full.at[src, pl.ds(o, w)], out.at[dst, pl.ds(o, w)])
        end = off + width
        early = [part(o, w) for o, w in ((0, off), (end, total - end)) if w]
        right = part(off, width)
        results.append((r, early, right))

        @pl.when(me == r)
        def _():
            if end < total:
                full[:, end:] = jnp.zeros((width, total - end), F32)
            for c in early:
                c.start()

    full[:, off : off + width] = jnp.zeros((width, width), F32)
    if not last:
        ih_out[...] = jnp.zeros((width, width), BF16)
        il_out[...] = jnp.zeros((width, width), BF16)
    cur[...] = diag[0:BLOCK, 0:BLOCK]
    blocks = width // BLOCK
    row = lax.broadcasted_iota(jnp.int32, (width, BLOCK), 0)
    col = lax.broadcasted_iota(jnp.int32, (BLOCK, width), 1)

    def inverse_rows(k):
        at = pl.multiple_of(k * BLOCK, BLOCK)
        here = pl.ds(at, BLOCK)
        left = jnp.where(col < at, full[here, off : off + width], 0.0)
        below = -dot3(split(left), (ih_out[...], il_out[...]), NN)
        rows = dot3((wh[...], wl[...]), split(below), NN)
        ih_out[here, :], il_out[here, :] = split(rows)
        ih_out[here, here], il_out[here, here] = wh[...], wl[...]

    def put_diagonal(k):
        at = pl.multiple_of(k * BLOCK, BLOCK)
        to = pl.ds(pl.multiple_of(off + at, BLOCK), BLOCK)
        full[pl.ds(at, BLOCK), to] = jnp.transpose(rprev[...])
        if not last:
            inverse_rows(k)

    def trailing(k):
        at = pl.multiple_of(k * BLOCK, BLOCK)
        column = dot3(split(diag[:, pl.ds(at, BLOCK)]), (wh[...], wl[...]), NT)
        column = jnp.where(row >= at + BLOCK, column, 0.0)
        c = split(column)
        diag[...] = diag[...] - dot3(c, c, NT)
        full[:, pl.ds(pl.multiple_of(off + at, BLOCK), BLOCK)] = column
        put_diagonal(k)

    def step(k, carry):
        at = pl.multiple_of(k * BLOCK, BLOCK)
        after = pl.multiple_of(jnp.minimum(at + BLOCK, width - BLOCK), BLOCK)
        w = factor_block(cur[...], comb, rout)
        new = split(w)
        trailing(jnp.maximum(k - 1, 0))
        wh[...], wl[...] = new
        rprev[...] = rout[...]
        c = split(dot3(split(diag[pl.ds(after, BLOCK), pl.ds(at, BLOCK)]), new, NT))
        cur[...] = diag[pl.ds(after, BLOCK), pl.ds(after, BLOCK)] - dot3(c, c, NT)
        return carry

    wh[...] = jnp.zeros((BLOCK, BLOCK), BF16)
    wl[...] = jnp.zeros((BLOCK, BLOCK), BF16)
    rprev[...] = jnp.zeros((BLOCK, BLOCK), F32)
    lax.fori_loop(0, blocks, step, 0)
    put_diagonal(blocks - 1)
    for r, early, right in results:

        @pl.when(me == r)
        def _():
            right.start()
            for c in early:
                c.wait()
            right.wait()


def band(plan, at_band, at_share, total, band_rows, vectors, out_so_far, pieces, held):
    off, width = plan[at_band]
    count, last = at_band, at_band + 1 == len(plan)
    depth = total_depth(pieces)
    any_spec = pl.BlockSpec(memory_space=pl.ANY)
    vm = pl.BlockSpec(memory_space=pltpu.VMEM)
    args, in_specs = [vectors], [vm]
    alias = {}
    if count:
        alias = {len(args): 0}
        args.append(out_so_far)
        in_specs.append(any_spec)
    xs, lhs, lls, ihs, ils = zip(*held) if held else ([],) * 5
    for group, spec in (
        (xs, vm), ([p for p, _ in pieces], any_spec), (lhs[1:], vm), (lls[1:], vm), (ihs, vm), (ils, vm)
    ):
        args += group
        in_specs += [spec] * len(group)
    left = max(off, BLOCK)
    vmem = pltpu.VMEM
    kept = [
        vmem((width, depth), BF16),
        vmem((width, left), BF16),
        vmem((width, left), BF16),
        vmem((width, width), BF16),
        vmem((width, width), BF16),
    ]
    out_shape = [jax.ShapeDtypeStruct((band_rows, total), F32)] + ([] if last else kept)
    copies = sum(1 if m is None else p.shape[0] for p, m in pieces)
    copies += 3 * (2 + width // band_rows)
    flops = 2 * width * (off + width) * depth + 6 * width * (off + width) ** 2
    return pl.pallas_call(
        functools.partial(band_kernel, plan, at_band, at_share, [m for _, m in pieces]),
        out_shape=out_shape,
        in_specs=in_specs,
        out_specs=[any_spec] + [vm] * (len(out_shape) - 1),
        scratch_shapes=(kept if last else [])
        + [
            vmem((width, left), F32),
            vmem((width, width), F32),
            vmem((BLOCK, BLOCK), F32),
            vmem((BLOCK, BLOCK), BF16),
            vmem((BLOCK, BLOCK), BF16),
            vmem((BLOCK, BLOCK), F32),
            vmem((BLOCK, BLOCK), F32),
            vmem((BLOCK, BLOCK), F32),
            vmem((width, total), F32),
            pltpu.SemaphoreType.DMA((copies,)),
        ],
        input_output_aliases=alias,
        cost_estimate=pl.CostEstimate(
            flops=flops, bytes_accessed=4 * width * total, transcendentals=0
        ),
        compiler_params=pltpu.CompilerParams(vmem_limit_bytes=VMEM_LIMIT),
        name="band_%d" % off,
    )(*args)


def total_depth(pieces):
    array = pieces[0][0]
    return array.shape[-1] * (array.shape[-3] if len(array.shape) > 2 else 1)


def gather_kernel(per_tile, widths, groups, info, returns, scale, onehot, *rest):
    outs, (held, left, made, sems) = rest[:-4], rest[-4:]
    rows, children = returns.shape[0], returns.shape[1]
    dests = outs[0].shape[0]
    copies = [
        pltpu.make_async_copy(
            returns.at[:, :, pl.ds(pl.multiple_of(info[2 * c], LANES), LANES)],
            held.at[c],
            sems.at[c],
        )
        for c in range(len(widths))
    ]
    for c in copies:
        c.start()
    span = per_tile * children
    tile = onehot.shape[1] // dests
    leaving = []
    for c, width in enumerate(widths):
        copies[c].wait()
        for k in range(rows):
            turned = jnp.transpose(held[c, k]).astype(F32) * scale[k : k + 1, :]
            left[c, :, k * children : (k + 1) * children] = turned.astype(BF16)
        picked = pl.ds(pl.multiple_of(info[2 * c + 1], width), width)
        for t in range(rows // per_tile):
            got = lax.dot_general(
                left[c, picked, t * span : (t + 1) * span], onehot[...], (NN, ((), ())),
                preferred_element_type=F32,
            ).astype(BF16)
            for d in range(dests):
                made[c, d, :width, t * tile : (t + 1) * tile] = got[:, d * tile : (d + 1) * tile]
        group, at = groups[c]
        leaving.append(
            pltpu.make_async_copy(
                made.at[c, :, pl.ds(0, width)],
                outs[group].at[:, pl.ds(at, width)],
                sems.at[len(widths) + c],
            )
        )
        leaving[-1].start()
    for c in leaving:
        c.wait()


def gather(returns, scale, onehot, firsts, widths, groups, dests, per_tile, capacity):
    rows, children, _ = returns.shape
    depth = capacity * rows
    info = jnp.stack([v for f in firsts for v in (f // LANES * LANES, f % LANES)])
    vm = pl.BlockSpec(memory_space=pltpu.VMEM)
    any_spec = pl.BlockSpec(memory_space=pl.ANY)
    bands = len(widths)
    sums = [sum(w for w, (h, _) in zip(widths, groups) if h == g) for g in range(groups[-1][0] + 1)]
    return pl.pallas_call(
        functools.partial(gather_kernel, per_tile, widths, groups),
        out_shape=[jax.ShapeDtypeStruct((dests, w, depth), BF16) for w in sums],
        in_specs=[pl.BlockSpec(memory_space=pltpu.SMEM), any_spec, vm, vm],
        out_specs=[any_spec] * len(sums),
        scratch_shapes=[
            pltpu.VMEM((bands, rows, children, LANES), BF16),
            pltpu.VMEM((bands, LANES, rows * children), BF16),
            pltpu.VMEM((bands, dests, max(widths), depth), BF16),
            pltpu.SemaphoreType.DMA((2 * bands,)),
        ],
        compiler_params=pltpu.CompilerParams(vmem_limit_bytes=GATHER_LIMIT),
        name="gather",
    )(info.astype(jnp.int32), returns, scale, onehot)


def after(value, *before):
    return lax.optimization_barrier((value,) + before)[0]


def round_sector(pieces, step):
    n = lax.axis_size("sector")
    turn = [(i, i ^ step) for i in range(n)]
    return pieces + [(lax.ppermute(p, "sector", turn), m | step) for p, m in pieces]


def band_plan(total, sector_count, node_count):
    width = sector_count * LANES
    plan = tuple((o, width) for o in range(0, total, width))
    half = max(1, len(plan) // GROUPS)
    return plan, tuple((b // half, b % half * LANES) for b in range(len(plan)))


def on_device(returns, barrier_scale, parent_ids, loadings, own_variance, sector_sizes):
    node_count = lax.axis_size("node")
    sector_count = lax.axis_size("sector")
    my_index = lax.axis_index("sector")
    child_count, row_count, asset_count = returns.shape
    capacity = max(2, 2 * child_count // node_count)
    band_rows = asset_count // sector_count
    in_pairs = (capacity * row_count) % LANES == 0 and sector_count & (sector_count - 1) == 0
    per_tile = row_count
    if LANES % capacity == 0 and row_count % (LANES // capacity) == 0:
        per_tile = LANES // capacity

    targets = parent_ids[:, 0]
    child_index = jnp.arange(child_count, dtype=jnp.int32)
    earlier = (targets[:, None] == targets[None, :]) & (child_index[None, :] < child_index[:, None])
    position = jnp.sum(earlier.astype(jnp.int32), axis=1)
    slot_of = targets * capacity + position
    dest = jnp.arange(node_count, dtype=jnp.int32)
    wanted = dest[:, None] * capacity + jnp.arange(capacity, dtype=jnp.int32)[None, :]
    tile_row = jnp.arange(per_tile, dtype=jnp.int32)
    onehot = (
        (slot_of[None, :, None, None, None] == wanted[None, None, :, None, :])
        & (tile_row[:, None, None, None, None] == tile_row[None, None, None, :, None])
    ).astype(BF16)
    onehot = onehot.reshape(per_tile * child_count, node_count * per_tile * capacity)
    by_row = returns.transpose(1, 0, 2)
    scale = jnp.sqrt(barrier_scale).T

    sector_ends = jnp.cumsum(sector_sizes)
    asset_index = jnp.arange(asset_count, dtype=jnp.int32)
    labels = jnp.sum((asset_index[:, None] >= sector_ends[None, :]).astype(jnp.int32), axis=1)
    vectors = jnp.concatenate([labels.astype(F32)[None, :], loadings, own_variance])
    vectors = jnp.pad(vectors, ((0, 8 - vectors.shape[0]), (0, 0)))

    plan, groups = band_plan(asset_count, sector_count, node_count)
    widths = [w // sector_count for _, w in plan]
    firsts = [off + my_index * w for (off, _), w in zip(plan, widths)]
    outgoing = gather(
        by_row, scale, onehot, firsts, widths, groups, node_count, per_tile, capacity
    )
    halves, held, outs = [], [], []
    per_group = len(plan) // len(outgoing)
    for at_band, (group, at) in enumerate(groups):
        for g in range(len(halves), min(group + LEAD, len(outgoing) - 1) + 1):
            outbox = after(outgoing[g], *(outs[-1:] if g >= LEAD else []))
            arrived = lax.all_to_all(outbox, "node", split_axis=0, concat_axis=0, tiled=True)
            pieces = [(arrived, 0)]
            halves.append(round_sector(pieces, sector_count // 2) if in_pairs else pieces)
        if at == 0:
            pieces, step = halves[group], sector_count // 4
            pieces = [(after(p, *outs[-1:]), m) for p, m in pieces]
            while in_pairs and step:
                pieces = round_sector(pieces, step)
                step //= 2
            if not in_pairs:
                pieces = [(lax.all_gather(pieces[0][0], "sector", axis=0), None)]
        mine = pieces
        if not in_pairs:
            share = pieces[0][0][:, :, at : at + widths[at_band]]
            mine = [(share.transpose(0, 2, 1, 3).reshape(plan[at_band][1], -1), None)]
        got = band(
            plan, at_band, at, asset_count, band_rows, vectors, outs[-1] if outs else None, mine, held
        )
        outs.append(got[0])
        held.append(got[1:])
    out = outs[-1]
    return out[None]


def solution(mesh):
    in_specs = (
        P("node", None, None),
        P("node", None),
        P("node", None),
        P("node", None),
        P("node", None),
        P(),
    )
    out_specs = P("node", "sector", None)
    return jax.shard_map(
        on_device, mesh=mesh, in_specs=in_specs, out_specs=out_specs, check_vma=False
    )
```

```python
import functools
import jax
import jax.numpy as jnp
from jax import lax
from jax.experimental import pallas as pl
from jax.experimental.pallas import tpu as pltpu
from jax.sharding import PartitionSpec as P

F32 = jnp.float32
BF16 = jnp.bfloat16
LANES = 128
BLOCK = 128
HALF = 64
VMEM_LIMIT = 28 * 2**20
GROUPS = 2
LEAD = 1
GATHER_LIMIT = 62 * 2**20


def split(x):
    high = x.astype(BF16)
    return high, (x - high.astype(F32)).astype(BF16)


def dot3(a, b, dims):
    one = lambda x, y: lax.dot_general(x, y, (dims, ((), ())), preferred_element_type=F32)
    (ah, al), (bh, bl) = a, b
    return one(ah, bh) + (one(ah, bl) + one(al, bh))


NT = ((1,), (1,))
TN = ((0,), (0,))
NN = ((1,), (0,))


def sweep_rows(rows_in, first, comb, rout):
    n = rows_in[0].shape[1]
    lane = lax.broadcasted_iota(jnp.int32, (8, n), 1)
    sub = lax.broadcasted_iota(jnp.int32, (8, n), 0)
    rows = list(rows_in)
    of_row = lambda v, i: jnp.broadcast_to(v[i : i + 1, :], (8, n))
    of_lane = lambda v, j: jnp.take_along_axis(v, jnp.full((8, n), j, jnp.int32), axis=1)
    both = (0, 1)
    for g in range(0, len(rows), 2):
        o = first + 8 * g
        cur = rows[g : g + 2]
        cols = [[of_lane(cur[q], o + j) for q in both] for j in range(16)]
        in_group = (lane >= o) & (lane < o + 16)
        raw = list(cur)
        unit = [jnp.where(lane == o + 8 * q + sub, 1.0, 0.0) for q in both]
        aug = [jnp.where(in_group, unit[q], cur[q]) for q in both]
        w_rows, r_rows = [None, None], [None, None]
        for x in range(0, 16, 2):
            y, h = x + 1, x // 8
            xs, ys = x % 8, y % 8
            a, b, c = of_row(cols[x][h], xs), of_row(cols[y][h], xs), of_row(cols[y][h], ys)
            inv_det = pltpu.reciprocal(a * c - b * b, approx=True)
            cx, cy = list(cols[x]), list(cols[y])
            cx[h] = jnp.where(sub == xs, -1.0, jnp.where(sub == ys, 0.0, cx[h]))
            cy[h] = jnp.where(sub == ys, -1.0, jnp.where(sub == xs, 0.0, cy[h]))
            mx = [inv_det * (c * cx[q] - b * cy[q]) for q in both]
            my = [inv_det * (a * cy[q] - b * cx[q]) for q in both]
            pair = (sub == xs) | (sub == ys)
            kept = lambda v, q: jnp.where(pair, 0.0, v) if q == h else v
            for l in range(y + 1, 16):
                ux, uy = of_row(cols[l][h], xs), of_row(cols[l][h], ys)
                cols[l] = [kept(cols[l][q], q) - (mx[q] * ux + my[q] * uy) for q in both]
            ra = lax.rsqrt(a)
            bra = b * ra
            rc = lax.rsqrt(c - bra * bra)
            scale = jnp.where(sub == xs, ra, rc)
            back = jnp.where(sub == xs, 0.0, bra) * ra
            ax, ay = of_row(aug[h], xs), of_row(aug[h], ys)
            rx, ry = of_row(raw[h], xs), of_row(raw[h], ys)
            wn = (aug[h] - back * ax) * scale
            rn = (raw[h] - back * rx) * scale
            w_rows[h] = wn if xs == 0 else jnp.where(sub >= xs, wn, w_rows[h])
            r_rows[h] = rn if xs == 0 else jnp.where(sub >= xs, rn, r_rows[h])
            aug = [kept(aug[q], q) - (mx[q] * ax + my[q] * ay) for q in both]
            raw = [raw[q] - (mx[q] * rx + my[q] * ry) if q >= h else raw[q] for q in both]
        for q in both:
            comb[o + 8 * q : o + 8 * q + 8, :] = w_rows[q]
            rout[o + 8 * q : o + 8 * q + 8, :] = jnp.where(lane >= o + 8 * q, r_rows[q], 0.0)
        solved = [of_row(aug[j // 8], j % 8) for j in range(16)]
        for h in range(g + 2, len(rows)):
            acc = [None, None]
            for j in range(16):
                t = of_lane(rows[h], o + j) * solved[j]
                acc[j % 2] = t if acc[j % 2] is None else acc[j % 2] + t
            rows[h] = jnp.where(in_group, 0.0, rows[h]) - (acc[0] + acc[1])


def factor_block(rest, comb, rout):
    n = BLOCK
    sweep_rows([rest[8 * h : 8 * h + 8, :] for h in range(HALF // 8)], 0, comb, rout)
    row = lax.broadcasted_iota(jnp.int32, (HALF, n), 0)
    lane = lax.broadcasted_iota(jnp.int32, (HALF, n), 1)
    top = jnp.where((lane < HALF) & (lane > row), 0.0, comb[0:HALF, :])
    low = jnp.where(lane < HALF, 0.0, rest[HALF:n, :])
    th, tl = split(top)
    low = low - dot3((th[:, HALF:], tl[:, HALF:]), (th, tl), TN)
    sweep_rows([low[8 * h : 8 * h + 8, :] for h in range(HALF // 8)], HALF, comb, rout)
    row = lax.broadcasted_iota(jnp.int32, (n, n), 0)
    lane = lax.broadcasted_iota(jnp.int32, (n, n), 1)
    return jnp.where(lane <= row, comb[...], 0.0)


def band_kernel(plan, at_band, at_share, masks, *refs):
    prior, (off, width) = plan[:at_band], plan[at_band]
    count, last = at_band, at_band + 1 == len(plan)
    it = iter(refs)
    take = lambda k: [next(it) for _ in range(k)]
    (vectors,) = take(1)
    out_in = take(1 if count else 0)
    xs = take(count)
    piece_hbm = take(len(masks))
    lhs, lls = [None] + take(max(count - 1, 0)), [None] + take(max(count - 1, 0))
    ihs, ils = take(count), take(count)
    (out,) = take(1)
    x_mine, ph, pl_, ih_out, il_out = take(5)
    mat, diag, cur, wh, wl, comb, rout, rprev, full, sems = take(10)
    me = lax.axis_index("sector")
    used = [0]

    def copy(src, dst):
        c = pltpu.make_async_copy(src, dst, sems.at[used[0]])
        used[0] += 1
        return c

    mine = []
    for ref, mask in zip(piece_hbm, masks):
        if mask is None:
            mine.append(copy(ref, x_mine))
        else:
            parts, part_depth = ref.shape[0], ref.shape[2]
            rows = width // lax.axis_size("sector")
            to = pl.ds(pl.multiple_of((me ^ mask) * rows, rows), rows)
            for d in range(parts):
                src = ref.at[d, pl.ds(at_share, rows)]
                mine.append(copy(src, x_mine.at[to, pl.ds(d * part_depth, part_depth)]))
    for c in mine:
        c.start()
    for c in mine:
        c.wait()

    turned = jnp.concatenate(
        [jnp.transpose(vectors[:, o : o + BLOCK]) for o in range(off, off + width, BLOCK)]
    )
    label_col, load_col, var_col = turned[:, 0:1], turned[:, 1:2], turned[:, 2:3]

    def normal_part(x, o, w):
        gram = lax.dot_general(x_mine[...], x, (NT, ((), ())), preferred_element_type=F32)
        same = label_col == vectors[0:1, o : o + w]
        return gram + jnp.where(same, load_col * vectors[1:2, o : o + w], 0.0)

    on_diag = lax.broadcasted_iota(jnp.int32, (width, width), 0) == lax.broadcasted_iota(
        jnp.int32, (width, width), 1
    )
    diag[...] = normal_part(x_mine[...], off, width) + jnp.where(on_diag, var_col, 0.0)
    for j in range(count):
        o, w = prior[j]
        mat[:, o : o + w] = normal_part(xs[j][...], o, w)
    for j in range(count):
        o, w = prior[j]
        acc = mat[:, o : o + w]
        if j > 0:
            acc = acc - dot3((ph[:, :o], pl_[:, :o]), (lhs[j][...], lls[j][...]), NT)
        part = dot3(split(acc), (ihs[j][...], ils[j][...]), NT)
        full[:, o : o + w] = part
        ph[:, o : o + w], pl_[:, o : o + w] = split(part)
    if count:
        diag[...] = diag[...] - dot3((ph[...], pl_[...]), (ph[...], pl_[...]), NT)

    total, band_rows = full.shape[1], out.shape[0]
    results = []
    for r in range(off // band_rows, (off + width - 1) // band_rows + 1):
        low, high = max(off, r * band_rows), min(off + width, (r + 1) * band_rows)
        src, dst = pl.ds(low - off, high - low), pl.ds(low - r * band_rows, high - low)
        part = lambda o, w: copy(full.at[src, pl.ds(o, w)], out.at[dst, pl.ds(o, w)])
        end = off + width
        early = [part(o, w) for o, w in ((0, off), (end, total - end)) if w]
        right = part(off, width)
        results.append((r, early, right))

        @pl.when(me == r)
        def _():
            if end < total:
                full[:, end:] = jnp.zeros((width, total - end), F32)
            for c in early:
                c.start()

    full[:, off : off + width] = jnp.zeros((width, width), F32)
    if not last:
        ih_out[...] = jnp.zeros((width, width), BF16)
        il_out[...] = jnp.zeros((width, width), BF16)
    cur[...] = diag[0:BLOCK, 0:BLOCK]
    blocks = width // BLOCK
    row = lax.broadcasted_iota(jnp.int32, (width, BLOCK), 0)
    col = lax.broadcasted_iota(jnp.int32, (BLOCK, width), 1)

    def inverse_rows(k):
        at = pl.multiple_of(k * BLOCK, BLOCK)
        here = pl.ds(at, BLOCK)
        left = jnp.where(col < at, full[here, off : off + width], 0.0)
        below = -dot3(split(left), (ih_out[...], il_out[...]), NN)
        rows = dot3((wh[...], wl[...]), split(below), NN)
        ih_out[here, :], il_out[here, :] = split(rows)
        ih_out[here, here], il_out[here, here] = wh[...], wl[...]

    def put_diagonal(k):
        at = pl.multiple_of(k * BLOCK, BLOCK)
        to = pl.ds(pl.multiple_of(off + at, BLOCK), BLOCK)
        lower = lax.broadcasted_iota(jnp.int32, (BLOCK, BLOCK), 0) >= lax.broadcasted_iota(
            jnp.int32, (BLOCK, BLOCK), 1
        )
        full[pl.ds(at, BLOCK), to] = jnp.where(lower, jnp.transpose(rprev[...]), 0.0)
        if not last:
            inverse_rows(k)

    def trailing(k):
        at = pl.multiple_of(k * BLOCK, BLOCK)
        column = dot3(split(diag[:, pl.ds(at, BLOCK)]), (wh[...], wl[...]), NT)
        column = jnp.where(row >= at + BLOCK, column, 0.0)
        c = split(column)
        diag[...] = diag[...] - dot3(c, c, NT)
        full[:, pl.ds(pl.multiple_of(off + at, BLOCK), BLOCK)] = column
        put_diagonal(k)

    def step(k, carry):
        at = pl.multiple_of(k * BLOCK, BLOCK)
        after = pl.multiple_of(jnp.minimum(at + BLOCK, width - BLOCK), BLOCK)
        w = factor_block(cur[...], comb, rout)
        new = split(w)
        trailing(jnp.maximum(k - 1, 0))
        wh[...], wl[...] = new
        rprev[...] = rout[...]
        c = split(dot3(split(diag[pl.ds(after, BLOCK), pl.ds(at, BLOCK)]), new, NT))
        cur[...] = diag[pl.ds(after, BLOCK), pl.ds(after, BLOCK)] - dot3(c, c, NT)
        return carry

    wh[...] = jnp.zeros((BLOCK, BLOCK), BF16)
    wl[...] = jnp.zeros((BLOCK, BLOCK), BF16)
    rprev[...] = jnp.zeros((BLOCK, BLOCK), F32)
    lax.fori_loop(0, blocks, step, 0)
    put_diagonal(blocks - 1)
    for r, early, right in results:

        @pl.when(me == r)
        def _():
            right.start()
            for c in early:
                c.wait()
            right.wait()


def band(plan, at_band, at_share, total, band_rows, vectors, out_so_far, pieces, held):
    off, width = plan[at_band]
    count, last = at_band, at_band + 1 == len(plan)
    depth = total_depth(pieces)
    any_spec = pl.BlockSpec(memory_space=pl.ANY)
    vm = pl.BlockSpec(memory_space=pltpu.VMEM)
    args, in_specs = [vectors], [vm]
    alias = {}
    if count:
        alias = {len(args): 0}
        args.append(out_so_far)
        in_specs.append(any_spec)
    xs, lhs, lls, ihs, ils = zip(*held) if held else ([],) * 5
    for group, spec in (
        (xs, vm), ([p for p, _ in pieces], any_spec), (lhs[1:], vm), (lls[1:], vm), (ihs, vm), (ils, vm)
    ):
        args += group
        in_specs += [spec] * len(group)
    left = max(off, BLOCK)
    vmem = pltpu.VMEM
    kept = [
        vmem((width, depth), BF16),
        vmem((width, left), BF16),
        vmem((width, left), BF16),
        vmem((width, width), BF16),
        vmem((width, width), BF16),
    ]
    out_shape = [jax.ShapeDtypeStruct((band_rows, total), F32)] + ([] if last else kept)
    copies = sum(1 if m is None else p.shape[0] for p, m in pieces)
    copies += 3 * (2 + width // band_rows)
    flops = 2 * width * (off + width) * depth + 6 * width * (off + width) ** 2
    return pl.pallas_call(
        functools.partial(band_kernel, plan, at_band, at_share, [m for _, m in pieces]),
        out_shape=out_shape,
        in_specs=in_specs,
        out_specs=[any_spec] + [vm] * (len(out_shape) - 1),
        scratch_shapes=(kept if last else [])
        + [
            vmem((width, left), F32),
            vmem((width, width), F32),
            vmem((BLOCK, BLOCK), F32),
            vmem((BLOCK, BLOCK), BF16),
            vmem((BLOCK, BLOCK), BF16),
            vmem((BLOCK, BLOCK), F32),
            vmem((BLOCK, BLOCK), F32),
            vmem((BLOCK, BLOCK), F32),
            vmem((width, total), F32),
            pltpu.SemaphoreType.DMA((copies,)),
        ],
        input_output_aliases=alias,
        cost_estimate=pl.CostEstimate(
            flops=flops, bytes_accessed=4 * width * total, transcendentals=0
        ),
        compiler_params=pltpu.CompilerParams(vmem_limit_bytes=VMEM_LIMIT),
        name="band_%d" % off,
    )(*args)


def total_depth(pieces):
    array = pieces[0][0]
    return array.shape[-1] * (array.shape[-3] if len(array.shape) > 2 else 1)


def gather_kernel(per_tile, widths, places, info, returns, scale, onehot, out, held, left, made, sems):
    rows, children = returns.shape[0], returns.shape[1]
    dests = out.shape[0]
    copies = [
        pltpu.make_async_copy(
            returns.at[:, :, pl.ds(pl.multiple_of(info[2 * c], LANES), LANES)],
            held.at[c],
            sems.at[c],
        )
        for c in range(len(widths))
    ]
    for c in copies:
        c.start()
    span = per_tile * children
    tile = onehot.shape[1] // dests
    leaving = []
    for c, width in enumerate(widths):
        copies[c].wait()
        for k in range(rows):
            turned = jnp.transpose(held[c, k]).astype(F32) * scale[k : k + 1, :]
            left[c, :, k * children : (k + 1) * children] = turned.astype(BF16)
        picked = pl.ds(pl.multiple_of(info[2 * c + 1], width), width)
        for t in range(rows // per_tile):
            got = lax.dot_general(
                left[c, picked, t * span : (t + 1) * span], onehot[...], (NN, ((), ())),
                preferred_element_type=F32,
            ).astype(BF16)
            for d in range(dests):
                made[c, d, :width, t * tile : (t + 1) * tile] = got[:, d * tile : (d + 1) * tile]
        leaving.append(
            pltpu.make_async_copy(
                made.at[c, :, pl.ds(0, width)],
                out.at[:, pl.ds(places[c], width)],
                sems.at[len(widths) + c],
            )
        )
        leaving[-1].start()
    for c in leaving:
        c.wait()


def gather(returns, scale, onehot, firsts, widths, dests, per_tile, capacity):
    rows, children, _ = returns.shape
    depth = capacity * rows
    info = jnp.stack([v for f in firsts for v in (f // LANES * LANES, f % LANES)])
    vm = pl.BlockSpec(memory_space=pltpu.VMEM)
    any_spec = pl.BlockSpec(memory_space=pl.ANY)
    bands = len(widths)
    places = [sum(widths[:b]) for b in range(bands)]
    return pl.pallas_call(
        functools.partial(gather_kernel, per_tile, widths, places),
        out_shape=jax.ShapeDtypeStruct((dests, sum(widths), depth), BF16),
        in_specs=[pl.BlockSpec(memory_space=pltpu.SMEM), any_spec, vm, vm],
        out_specs=any_spec,
        scratch_shapes=[
            pltpu.VMEM((bands, rows, children, LANES), BF16),
            pltpu.VMEM((bands, LANES, rows * children), BF16),
            pltpu.VMEM((bands, dests, max(widths), depth), BF16),
            pltpu.SemaphoreType.DMA((2 * bands,)),
        ],
        compiler_params=pltpu.CompilerParams(vmem_limit_bytes=GATHER_LIMIT),
        name="gather",
    )(info.astype(jnp.int32), returns, scale, onehot)


def after(value, *before):
    return lax.optimization_barrier((value,) + before)[0]


def round_sector(pieces, step):
    n = lax.axis_size("sector")
    turn = [(i, i ^ step) for i in range(n)]
    return pieces + [(lax.ppermute(p, "sector", turn), m | step) for p, m in pieces]


def band_plan(total, sector_count, node_count):
    width = sector_count * LANES
    plan = tuple((o, width) for o in range(0, total, width))
    half = max(1, len(plan) // GROUPS)
    return plan, tuple((b // half, b % half * LANES) for b in range(len(plan)))


def on_device(returns, barrier_scale, parent_ids, loadings, own_variance, sector_sizes):
    node_count = lax.axis_size("node")
    sector_count = lax.axis_size("sector")
    my_index = lax.axis_index("sector")
    child_count, row_count, asset_count = returns.shape
    capacity = max(2, 2 * child_count // node_count)
    band_rows = asset_count // sector_count
    in_pairs = (capacity * row_count) % LANES == 0 and sector_count & (sector_count - 1) == 0
    per_tile = row_count
    if LANES % capacity == 0 and row_count % (LANES // capacity) == 0:
        per_tile = LANES // capacity

    targets = parent_ids[:, 0]
    child_index = jnp.arange(child_count, dtype=jnp.int32)
    earlier = (targets[:, None] == targets[None, :]) & (child_index[None, :] < child_index[:, None])
    position = jnp.sum(earlier.astype(jnp.int32), axis=1)
    slot_of = targets * capacity + position
    lane = jnp.arange(node_count * per_tile * capacity, dtype=jnp.int32)
    wanted = lane // (per_tile * capacity) * capacity + lane % capacity
    tile_row = lane // capacity % per_tile
    child_tile = jnp.arange(per_tile * child_count, dtype=jnp.int32) // child_count
    onehot = (
        (jnp.tile(slot_of, per_tile)[:, None] == wanted[None, :])
        & (child_tile[:, None] == tile_row[None, :])
    ).astype(BF16)
    by_row = returns.transpose(1, 0, 2)
    scale = jnp.sqrt(barrier_scale).T

    sector_ends = jnp.cumsum(sector_sizes)
    asset_index = jnp.arange(asset_count, dtype=jnp.int32)
    labels = jnp.sum((asset_index[:, None] >= sector_ends[None, :]).astype(jnp.int32), axis=1)
    vectors = jnp.concatenate([labels.astype(F32)[None, :], loadings, own_variance])
    vectors = jnp.pad(vectors, ((0, 8 - vectors.shape[0]), (0, 0)))

    plan, groups = band_plan(asset_count, sector_count, node_count)
    widths = [w // sector_count for _, w in plan]
    firsts = [off + my_index * w for (off, _), w in zip(plan, widths)]
    outgoing = []
    for g in range(groups[-1][0] + 1):
        mine = [b for b in range(len(plan)) if groups[b][0] == g]
        outgoing.append(
            gather(
                after(by_row, *outgoing[-1:]), scale, onehot, [firsts[b] for b in mine],
                [widths[b] for b in mine], node_count, per_tile, capacity,
            )
        )
    halves, held, outs = [], [], []
    for at_band, (group, at) in enumerate(groups):
        for b in range(len(halves), min(at_band + LEAD, len(plan) - 1) + 1):
            g, place = groups[b]
            if place == 0:
                arrived = lax.all_to_all(
                    outgoing[g], "node", split_axis=0, concat_axis=0, tiled=True
                )
                if g:
                    arrived = after(arrived, *outs[-1:])
            pieces = [(arrived[:, place : place + widths[b]], 0)]
            halves.append(round_sector(pieces, sector_count // 2) if in_pairs else pieces)
        pieces, step = halves[at_band], sector_count // 4
        pieces = [(after(p, *outs[-1:]), m) for p, m in pieces]
        if in_pairs:
            while step:
                pieces = round_sector(pieces, step)
                step //= 2
        else:
            share = lax.all_gather(pieces[0][0], "sector", axis=0)
            pieces = [(share.transpose(0, 2, 1, 3).reshape(plan[at_band][1], -1), None)]
        got = band(
            plan, at_band, 0, asset_count, band_rows, vectors, outs[-1] if outs else None, pieces, held
        )
        outs.append(got[0])
        held.append(got[1:])
    out = outs[-1]
    return out[None]


def solution(mesh):
    in_specs = (
        P("node", None, None),
        P("node", None),
        P("node", None),
        P("node", None),
        P("node", None),
        P(),
    )
    out_specs = P("node", "sector", None)
    return jax.shard_map(
        on_device, mesh=mesh, in_specs=in_specs, out_specs=out_specs, check_vma=False
    )
```

```python
import functools
import jax
import jax.numpy as jnp
from jax import lax
from jax.experimental import pallas as pl
from jax.experimental.pallas import tpu as pltpu
from jax.sharding import PartitionSpec as P

F32 = jnp.float32
BF16 = jnp.bfloat16
LANES = 128
BLOCK = 128
HALF = 64
VMEM_LIMIT = 28 * 2**20
GROUPS = 2
LEAD = 1
GATHER_LIMIT = 62 * 2**20


def split(x):
    high = x.astype(BF16)
    return high, (x - high.astype(F32)).astype(BF16)


def dot3(a, b, dims):
    one = lambda x, y: lax.dot_general(x, y, (dims, ((), ())), preferred_element_type=F32)
    (ah, al), (bh, bl) = a, b
    return one(ah, bh) + (one(ah, bl) + one(al, bh))


NT = ((1,), (1,))
TN = ((0,), (0,))
NN = ((1,), (0,))


def sweep_rows(rows_in, first, comb, rout):
    n = rows_in[0].shape[1]
    lane = lax.broadcasted_iota(jnp.int32, (8, n), 1)
    sub = lax.broadcasted_iota(jnp.int32, (8, n), 0)
    rows = list(rows_in)
    of_row = lambda v, i: jnp.broadcast_to(v[i : i + 1, :], (8, n))
    of_lane = lambda v, j: jnp.take_along_axis(v, jnp.full((8, n), j, jnp.int32), axis=1)
    both = (0, 1)
    for g in range(0, len(rows), 2):
        o = first + 8 * g
        cur = rows[g : g + 2]
        cols = [[of_lane(cur[q], o + j) for q in both] for j in range(16)]
        in_group = (lane >= o) & (lane < o + 16)
        raw = list(cur)
        unit = [jnp.where(lane == o + 8 * q + sub, 1.0, 0.0) for q in both]
        aug = [jnp.where(in_group, unit[q], cur[q]) for q in both]
        w_rows, r_rows = [None, None], [None, None]
        for x in range(0, 16, 2):
            y, h = x + 1, x // 8
            xs, ys = x % 8, y % 8
            a, b, c = of_row(cols[x][h], xs), of_row(cols[y][h], xs), of_row(cols[y][h], ys)
            inv_det = pltpu.reciprocal(a * c - b * b, approx=True)
            cx, cy = list(cols[x]), list(cols[y])
            cx[h] = jnp.where(sub == xs, -1.0, jnp.where(sub == ys, 0.0, cx[h]))
            cy[h] = jnp.where(sub == ys, -1.0, jnp.where(sub == xs, 0.0, cy[h]))
            mx = [inv_det * (c * cx[q] - b * cy[q]) for q in both]
            my = [inv_det * (a * cy[q] - b * cx[q]) for q in both]
            pair = (sub == xs) | (sub == ys)
            kept = lambda v, q: jnp.where(pair, 0.0, v) if q == h else v
            for l in range(y + 1, 16):
                ux, uy = of_row(cols[l][h], xs), of_row(cols[l][h], ys)
                cols[l] = [kept(cols[l][q], q) - (mx[q] * ux + my[q] * uy) for q in both]
            ra = lax.rsqrt(a)
            bra = b * ra
            rc = lax.rsqrt(c - bra * bra)
            scale = jnp.where(sub == xs, ra, rc)
            back = jnp.where(sub == xs, 0.0, bra) * ra
            ax, ay = of_row(aug[h], xs), of_row(aug[h], ys)
            rx, ry = of_row(raw[h], xs), of_row(raw[h], ys)
            wn = (aug[h] - back * ax) * scale
            rn = (raw[h] - back * rx) * scale
            w_rows[h] = wn if xs == 0 else jnp.where(sub >= xs, wn, w_rows[h])
            r_rows[h] = rn if xs == 0 else jnp.where(sub >= xs, rn, r_rows[h])
            aug = [kept(aug[q], q) - (mx[q] * ax + my[q] * ay) for q in both]
            raw = [raw[q] - (mx[q] * rx + my[q] * ry) if q >= h else raw[q] for q in both]
        for q in both:
            comb[o + 8 * q : o + 8 * q + 8, :] = w_rows[q]
            rout[o + 8 * q : o + 8 * q + 8, :] = jnp.where(lane >= o + 8 * q, r_rows[q], 0.0)
        solved = [of_row(aug[j // 8], j % 8) for j in range(16)]
        for h in range(g + 2, len(rows)):
            acc = [None, None]
            for j in range(16):
                t = of_lane(rows[h], o + j) * solved[j]
                acc[j % 2] = t if acc[j % 2] is None else acc[j % 2] + t
            rows[h] = jnp.where(in_group, 0.0, rows[h]) - (acc[0] + acc[1])


def factor_block(rest, comb, rout):
    n = BLOCK
    sweep_rows([rest[8 * h : 8 * h + 8, :] for h in range(HALF // 8)], 0, comb, rout)
    row = lax.broadcasted_iota(jnp.int32, (HALF, n), 0)
    lane = lax.broadcasted_iota(jnp.int32, (HALF, n), 1)
    top = jnp.where((lane < HALF) & (lane > row), 0.0, comb[0:HALF, :])
    low = jnp.where(lane < HALF, 0.0, rest[HALF:n, :])
    th, tl = split(top)
    low = low - dot3((th[:, HALF:], tl[:, HALF:]), (th, tl), TN)
    sweep_rows([low[8 * h : 8 * h + 8, :] for h in range(HALF // 8)], HALF, comb, rout)
    row = lax.broadcasted_iota(jnp.int32, (n, n), 0)
    lane = lax.broadcasted_iota(jnp.int32, (n, n), 1)
    return jnp.where(lane <= row, comb[...], 0.0)


def band_kernel(plan, at_band, at_share, masks, *refs):
    prior, (off, width) = plan[:at_band], plan[at_band]
    count, last = at_band, at_band + 1 == len(plan)
    it = iter(refs)
    take = lambda k: [next(it) for _ in range(k)]
    (vectors,) = take(1)
    out_in = take(1 if count else 0)
    xs = take(count)
    piece_hbm = take(len(masks))
    lhs, lls = [None] + take(max(count - 1, 0)), [None] + take(max(count - 1, 0))
    ihs, ils = take(count), take(count)
    (out,) = take(1)
    x_mine, ph, pl_, ih_out, il_out = take(5)
    mat, diag, cur, wh, wl, comb, rout, rprev, full, sems = take(10)
    me = lax.axis_index("sector")
    used = [0]

    def copy(src, dst):
        c = pltpu.make_async_copy(src, dst, sems.at[used[0]])
        used[0] += 1
        return c

    mine = []
    for ref, mask in zip(piece_hbm, masks):
        if mask is None:
            mine.append(copy(ref, x_mine))
        else:
            parts, part_depth = ref.shape[0], ref.shape[2]
            rows = width // lax.axis_size("sector")
            to = pl.ds(pl.multiple_of((me ^ mask) * rows, rows), rows)
            for d in range(parts):
                src = ref.at[d, pl.ds(at_share, rows)]
                mine.append(copy(src, x_mine.at[to, pl.ds(d * part_depth, part_depth)]))
    for c in mine:
        c.start()
    for c in mine:
        c.wait()

    turned = jnp.concatenate(
        [jnp.transpose(vectors[:, o : o + BLOCK]) for o in range(off, off + width, BLOCK)]
    )
    label_col, load_col, var_col = turned[:, 0:1], turned[:, 1:2], turned[:, 2:3]

    def normal_part(x, o, w, top=0):
        gram = lax.dot_general(x_mine[top:, :], x, (NT, ((), ())), preferred_element_type=F32)
        same = label_col[top:] == vectors[0:1, o : o + w]
        return gram + jnp.where(same, load_col[top:] * vectors[1:2, o : o + w], 0.0)

    on_diag = lax.broadcasted_iota(jnp.int32, (width, width), 0) == lax.broadcasted_iota(
        jnp.int32, (width, width), 1
    )
    half = width // 2
    own = jnp.where(on_diag, var_col, 0.0)
    diag[:half, half:] = jnp.zeros((half, width - half), F32)
    diag[:, :half] = normal_part(x_mine[:half, :], off, half) + own[:, :half]
    low = normal_part(x_mine[half:, :], off + half, width - half, half)
    diag[half:, half:] = low + own[half:, half:]
    for j in range(count):
        o, w = prior[j]
        mat[:, o : o + w] = normal_part(xs[j][...], o, w)
    for j in range(count):
        o, w = prior[j]
        acc = mat[:, o : o + w]
        if j > 0:
            acc = acc - dot3((ph[:, :o], pl_[:, :o]), (lhs[j][...], lls[j][...]), NT)
        part = dot3(split(acc), (ihs[j][...], ils[j][...]), NT)
        full[:, o : o + w] = part
        ph[:, o : o + w], pl_[:, o : o + w] = split(part)
    if count:
        upper, lower = (ph[:half, :], pl_[:half, :]), (ph[half:, :], pl_[half:, :])
        diag[:, :half] = diag[:, :half] - dot3((ph[...], pl_[...]), upper, NT)
        diag[half:, half:] = diag[half:, half:] - dot3(lower, lower, NT)

    total, band_rows = full.shape[1], out.shape[0]
    results = []
    for r in range(off // band_rows, (off + width - 1) // band_rows + 1):
        low, high = max(off, r * band_rows), min(off + width, (r + 1) * band_rows)
        src, dst = pl.ds(low - off, high - low), pl.ds(low - r * band_rows, high - low)
        part = lambda o, w: copy(full.at[src, pl.ds(o, w)], out.at[dst, pl.ds(o, w)])
        end = off + width
        early = [part(o, w) for o, w in ((0, off), (end, total - end)) if w]
        right = part(off, width)
        results.append((r, early, right))

        @pl.when(me == r)
        def _():
            if end < total:
                full[:, end:] = jnp.zeros((width, total - end), F32)
            for c in early:
                c.start()

    full[:, off : off + width] = jnp.zeros((width, width), F32)
    if not last:
        ih_out[...] = jnp.zeros((width, width), BF16)
        il_out[...] = jnp.zeros((width, width), BF16)
    cur[...] = diag[0:BLOCK, 0:BLOCK]
    blocks = width // BLOCK
    row = lax.broadcasted_iota(jnp.int32, (width, BLOCK), 0)
    col = lax.broadcasted_iota(jnp.int32, (BLOCK, width), 1)

    def inverse_rows(k):
        at = pl.multiple_of(k * BLOCK, BLOCK)
        here = pl.ds(at, BLOCK)
        left = jnp.where(col < at, full[here, off : off + width], 0.0)
        below = -dot3(split(left), (ih_out[...], il_out[...]), NN)
        rows = dot3((wh[...], wl[...]), split(below), NN)
        ih_out[here, :], il_out[here, :] = split(rows)
        ih_out[here, here], il_out[here, here] = wh[...], wl[...]

    def put_diagonal(k):
        at = pl.multiple_of(k * BLOCK, BLOCK)
        to = pl.ds(pl.multiple_of(off + at, BLOCK), BLOCK)
        lower = lax.broadcasted_iota(jnp.int32, (BLOCK, BLOCK), 0) >= lax.broadcasted_iota(
            jnp.int32, (BLOCK, BLOCK), 1
        )
        full[pl.ds(at, BLOCK), to] = jnp.where(lower, jnp.transpose(rprev[...]), 0.0)
        if not last:
            inverse_rows(k)

    def trailing(k):
        at = pl.multiple_of(k * BLOCK, BLOCK)
        column = dot3(split(diag[:, pl.ds(at, BLOCK)]), (wh[...], wl[...]), NT)
        column = jnp.where(row >= at + BLOCK, column, 0.0)
        c = split(column)
        diag[...] = diag[...] - dot3(c, c, NT)
        full[:, pl.ds(pl.multiple_of(off + at, BLOCK), BLOCK)] = column
        put_diagonal(k)

    def step(k, carry):
        at = pl.multiple_of(k * BLOCK, BLOCK)
        after = pl.multiple_of(jnp.minimum(at + BLOCK, width - BLOCK), BLOCK)
        w = factor_block(cur[...], comb, rout)
        new = split(w)
        trailing(jnp.maximum(k - 1, 0))
        wh[...], wl[...] = new
        rprev[...] = rout[...]
        c = split(dot3(split(diag[pl.ds(after, BLOCK), pl.ds(at, BLOCK)]), new, NT))
        cur[...] = diag[pl.ds(after, BLOCK), pl.ds(after, BLOCK)] - dot3(c, c, NT)
        return carry

    wh[...] = jnp.zeros((BLOCK, BLOCK), BF16)
    wl[...] = jnp.zeros((BLOCK, BLOCK), BF16)
    rprev[...] = jnp.zeros((BLOCK, BLOCK), F32)
    lax.fori_loop(0, blocks, step, 0)
    put_diagonal(blocks - 1)
    for r, early, right in results:

        @pl.when(me == r)
        def _():
            right.start()
            for c in early:
                c.wait()
            right.wait()


def band(plan, at_band, at_share, total, band_rows, vectors, out_so_far, pieces, held):
    off, width = plan[at_band]
    count, last = at_band, at_band + 1 == len(plan)
    depth = total_depth(pieces)
    any_spec = pl.BlockSpec(memory_space=pl.ANY)
    vm = pl.BlockSpec(memory_space=pltpu.VMEM)
    args, in_specs = [vectors], [vm]
    alias = {}
    if count:
        alias = {len(args): 0}
        args.append(out_so_far)
        in_specs.append(any_spec)
    xs, lhs, lls, ihs, ils = zip(*held) if held else ([],) * 5
    for group, spec in (
        (xs, vm), ([p for p, _ in pieces], any_spec), (lhs[1:], vm), (lls[1:], vm), (ihs, vm), (ils, vm)
    ):
        args += group
        in_specs += [spec] * len(group)
    left = max(off, BLOCK)
    vmem = pltpu.VMEM
    kept = [
        vmem((width, depth), BF16),
        vmem((width, left), BF16),
        vmem((width, left), BF16),
        vmem((width, width), BF16),
        vmem((width, width), BF16),
    ]
    out_shape = [jax.ShapeDtypeStruct((band_rows, total), F32)] + ([] if last else kept)
    copies = sum(1 if m is None else p.shape[0] for p, m in pieces)
    copies += 3 * (2 + width // band_rows)
    flops = 2 * width * (off + width) * depth + 6 * width * (off + width) ** 2
    return pl.pallas_call(
        functools.partial(band_kernel, plan, at_band, at_share, [m for _, m in pieces]),
        out_shape=out_shape,
        in_specs=in_specs,
        out_specs=[any_spec] + [vm] * (len(out_shape) - 1),
        scratch_shapes=(kept if last else [])
        + [
            vmem((width, left), F32),
            vmem((width, width), F32),
            vmem((BLOCK, BLOCK), F32),
            vmem((BLOCK, BLOCK), BF16),
            vmem((BLOCK, BLOCK), BF16),
            vmem((BLOCK, BLOCK), F32),
            vmem((BLOCK, BLOCK), F32),
            vmem((BLOCK, BLOCK), F32),
            vmem((width, total), F32),
            pltpu.SemaphoreType.DMA((copies,)),
        ],
        input_output_aliases=alias,
        cost_estimate=pl.CostEstimate(
            flops=flops, bytes_accessed=4 * width * total, transcendentals=0
        ),
        compiler_params=pltpu.CompilerParams(vmem_limit_bytes=VMEM_LIMIT),
        name="band_%d" % off,
    )(*args)


def total_depth(pieces):
    array = pieces[0][0]
    return array.shape[-1] * (array.shape[-3] if len(array.shape) > 2 else 1)


def gather_kernel(per_tile, widths, places, info, returns, scale, onehot, out, held, left, made, sems):
    rows, children = returns.shape[0], returns.shape[1]
    dests = out.shape[0]
    copies = [
        pltpu.make_async_copy(
            returns.at[:, :, pl.ds(pl.multiple_of(info[2 * c], LANES), LANES)],
            held.at[c],
            sems.at[c],
        )
        for c in range(len(widths))
    ]
    for c in copies:
        c.start()
    span = per_tile * children
    tile = onehot.shape[1] // dests
    leaving = []
    for c, width in enumerate(widths):
        copies[c].wait()
        for k in range(rows):
            turned = jnp.transpose(held[c, k]).astype(F32) * scale[k : k + 1, :]
            left[c, :, k * children : (k + 1) * children] = turned.astype(BF16)
        picked = pl.ds(pl.multiple_of(info[2 * c + 1], width), width)
        for t in range(rows // per_tile):
            got = lax.dot_general(
                left[c, picked, t * span : (t + 1) * span], onehot[...], (NN, ((), ())),
                preferred_element_type=F32,
            ).astype(BF16)
            for d in range(dests):
                made[c, d, :width, t * tile : (t + 1) * tile] = got[:, d * tile : (d + 1) * tile]
        leaving.append(
            pltpu.make_async_copy(
                made.at[c, :, pl.ds(0, width)],
                out.at[:, pl.ds(places[c], width)],
                sems.at[len(widths) + c],
            )
        )
        leaving[-1].start()
    for c in leaving:
        c.wait()


def gather(returns, scale, onehot, firsts, widths, dests, per_tile, capacity):
    rows, children, _ = returns.shape
    depth = capacity * rows
    info = jnp.stack([v for f in firsts for v in (f // LANES * LANES, f % LANES)])
    vm = pl.BlockSpec(memory_space=pltpu.VMEM)
    any_spec = pl.BlockSpec(memory_space=pl.ANY)
    bands = len(widths)
    places = [sum(widths[:b]) for b in range(bands)]
    return pl.pallas_call(
        functools.partial(gather_kernel, per_tile, widths, places),
        out_shape=jax.ShapeDtypeStruct((dests, sum(widths), depth), BF16),
        in_specs=[pl.BlockSpec(memory_space=pltpu.SMEM), any_spec, vm, vm],
        out_specs=any_spec,
        scratch_shapes=[
            pltpu.VMEM((bands, rows, children, LANES), BF16),
            pltpu.VMEM((bands, LANES, rows * children), BF16),
            pltpu.VMEM((bands, dests, max(widths), depth), BF16),
            pltpu.SemaphoreType.DMA((2 * bands,)),
        ],
        compiler_params=pltpu.CompilerParams(vmem_limit_bytes=GATHER_LIMIT),
        name="gather",
    )(info.astype(jnp.int32), returns, scale, onehot)


def after(value, *before):
    return lax.optimization_barrier((value,) + before)[0]


def round_sector(pieces, step):
    n = lax.axis_size("sector")
    turn = [(i, i ^ step) for i in range(n)]
    return pieces + [(lax.ppermute(p, "sector", turn), m | step) for p, m in pieces]


def band_plan(total, sector_count, node_count):
    width = sector_count * LANES
    plan = tuple((o, width) for o in range(0, total, width))
    half = max(1, len(plan) // GROUPS)
    return plan, tuple((b // half, b % half * LANES) for b in range(len(plan)))


def on_device(returns, barrier_scale, parent_ids, loadings, own_variance, sector_sizes):
    node_count = lax.axis_size("node")
    sector_count = lax.axis_size("sector")
    my_index = lax.axis_index("sector")
    child_count, row_count, asset_count = returns.shape
    capacity = max(2, 2 * child_count // node_count)
    band_rows = asset_count // sector_count
    in_pairs = (capacity * row_count) % LANES == 0 and sector_count & (sector_count - 1) == 0
    per_tile = row_count
    if LANES % capacity == 0 and row_count % (LANES // capacity) == 0:
        per_tile = LANES // capacity

    targets = parent_ids[:, 0]
    child_index = jnp.arange(child_count, dtype=jnp.int32)
    earlier = (targets[:, None] == targets[None, :]) & (child_index[None, :] < child_index[:, None])
    position = jnp.sum(earlier.astype(jnp.int32), axis=1)
    slot_of = targets * capacity + position
    lane = jnp.arange(node_count * per_tile * capacity, dtype=jnp.int32)
    wanted = lane // (per_tile * capacity) * capacity + lane % capacity
    tile_row = lane // capacity % per_tile
    child_tile = jnp.arange(per_tile * child_count, dtype=jnp.int32) // child_count
    onehot = (
        (jnp.tile(slot_of, per_tile)[:, None] == wanted[None, :])
        & (child_tile[:, None] == tile_row[None, :])
    ).astype(BF16)
    by_row = returns.transpose(1, 0, 2)
    scale = jnp.sqrt(barrier_scale).T

    sector_ends = jnp.cumsum(sector_sizes)
    asset_index = jnp.arange(asset_count, dtype=jnp.int32)
    labels = jnp.sum((asset_index[:, None] >= sector_ends[None, :]).astype(jnp.int32), axis=1)
    vectors = jnp.concatenate([labels.astype(F32)[None, :], loadings, own_variance])
    vectors = jnp.pad(vectors, ((0, 8 - vectors.shape[0]), (0, 0)))

    plan, groups = band_plan(asset_count, sector_count, node_count)
    widths = [w // sector_count for _, w in plan]
    firsts = [off + my_index * w for (off, _), w in zip(plan, widths)]
    outgoing = []
    for g in range(groups[-1][0] + 1):
        mine = [b for b in range(len(plan)) if groups[b][0] == g]
        outgoing.append(
            gather(
                after(by_row, *outgoing[-1:]), scale, onehot, [firsts[b] for b in mine],
                [widths[b] for b in mine], node_count, per_tile, capacity,
            )
        )
    halves, held, outs = [], [], []
    for at_band, (group, at) in enumerate(groups):
        for b in range(len(halves), min(at_band + LEAD, len(plan) - 1) + 1):
            g, place = groups[b]
            if place == 0:
                arrived = lax.all_to_all(
                    outgoing[g], "node", split_axis=0, concat_axis=0, tiled=True
                )
                if g:
                    arrived = after(arrived, *outs[-1:])
            pieces = [(arrived[:, place : place + widths[b]], 0)]
            halves.append(round_sector(pieces, sector_count // 2) if in_pairs else pieces)
        pieces, step = halves[at_band], sector_count // 4
        pieces = [(after(p, *outs[-1:]), m) for p, m in pieces]
        if in_pairs:
            while step:
                pieces = round_sector(pieces, step)
                step //= 2
        else:
            share = lax.all_gather(pieces[0][0], "sector", axis=0)
            pieces = [(share.transpose(0, 2, 1, 3).reshape(plan[at_band][1], -1), None)]
        got = band(
            plan, at_band, 0, asset_count, band_rows, vectors, outs[-1] if outs else None, pieces, held
        )
        outs.append(got[0])
        held.append(got[1:])
    out = outs[-1]
    return out[None]


def solution(mesh):
    in_specs = (
        P("node", None, None),
        P("node", None),
        P("node", None),
        P("node", None),
        P("node", None),
        P(),
    )
    out_specs = P("node", "sector", None)
    return jax.shard_map(
        on_device, mesh=mesh, in_specs=in_specs, out_specs=out_specs, check_vma=False
    )
```
